32 devices in a mesh: pairs: 16 (over z, y, x), aux: 2 (over core).
Axes of the slice: x: 2, y: 2, z: 4, core: 2. Of those that a mesh axis runs over, the one named last changes fastest.
Arguments:
- amplitudes: bfloat16 [256, 128, 128], P('pairs'), may hold values from -6 to 6
- pno_coef: bfloat16 [256, 256, 128], P('pairs'), may hold values from -0.75 to 0.75
- ladder_ints: bfloat16 [320, 128, 128], P('aux'), may hold values from -0.3125 to 0.3125
- coulomb_ints: bfloat16 [256, 128, 128], P(('pairs', 'aux')), may hold values from -6 to 6
- pno_energy: float32 [256, 128], P(('pairs', 'aux')), may hold values from 0.3 to 3
- link_owner: int32 [3072, 1], P(('pairs', 'aux')), may hold values from 0 to 15; in each aligned block of 96 rows (0 to 95, 96 to 191, ...) at most 8 rows name the same one
- link_local: int32 [3072, 1], P(('pairs', 'aux')), may hold values from 0 to 15
Outputs:
- updated: float32 [256, 128, 128], P(('pairs', 'aux'))
The draws below stay inside these ranges and needn't reach their ends.
Inputs may be any that keep to these rules, and one draw needn't show every extreme that they name: `link_owner`: in each device's aligned block of 96 rows no owner group is named by more than 8 rows, a bound that some block reaches.
All inputs are finite; a program needn't handle non-finite values.
Results may differ from the reference program's by a relative error of at most 0.0033.
Values may be sent and summed in bfloat16 or wider, within the bound.
A program may use at most 128 MiB of HBM per device.

```python
import math
import jax
import jax.numpy as jnp
import numpy as np
from jax import lax

NPNO = 128
NPAO = 256
NAUXF = 320
PAIR_DEV = 16
LPS = 6
PAIRS = 256
LINKS = 12
SLOTS = 96
CAP = 8
LINK_ROWS = 3072
N_PAIRS = 16
N_AUX = 2


def place_ends(values, rng, smallest, high):
    place = [jax.random.randint(jax.random.fold_in(rng, axis), (), 0, length) for axis, length in enumerate(values.shape)]
    longest = values.shape.index(max(values.shape))
    neighbour = place[:longest] + [(place[longest] + 1) % values.shape[longest]] + place[longest + 1:]
    return values.at[tuple(place)].set(smallest).at[tuple(neighbour)].set(high)


def level_of(stream_key, shape, shards, least, high):
    level, own = 1.0, jax.random.fold_in(stream_key, 6)
    for position, parts in shards:
        heights = jnp.exp(jax.random.uniform(jax.random.fold_in(own, position), (parts,), jnp.float32, least / len(shards), high / len(shards)))
        level = level * jnp.repeat(heights, shape[position] // parts).reshape([-1 if axis == position else 1 for axis in range(len(shape))])
    return level


def routed_block(rng, own, number, rows, amount, top, bound, skew):
    order = jax.random.permutation(rng, amount)
    heavy_load, ordinary = shares(amount, rows * top, bound, skew, True), shares(amount, rows * top, bound, skew, False)
    places = jnp.arange(amount)

    def named(lengths, turn):
        used = int((lengths > 0).sum())
        fixed = max(1, used // 4)
        moved = fixed + (places - fixed + turn * (used - fixed)) % max(1, amount - fixed)
        return jnp.zeros((amount,), jnp.int32).at[order[jnp.where(places < fixed, places, moved)]].set(jnp.asarray(lengths, jnp.int32))

    lengths = jnp.where(number % 4 == 0, named(heavy_load, number // 4), named(ordinary, number - number // 4 - 1))
    mixed = jax.random.permutation(jax.random.fold_in(own, 3), amount)
    source_of, sink = mixed[0:amount // 2 * 2:2], mixed[1:amount // 2 * 2:2]
    slack = jnp.minimum(lengths[source_of] - 1, bound - lengths[sink]) // 2
    slack = jnp.where((source_of == order[0]) | (sink == order[0]) | (lengths[sink] == 0), 0, jnp.maximum(slack, 0))
    moved = jax.random.randint(jax.random.fold_in(own, 4), (amount // 2,), 0, 1 << 20) % (slack + 1)
    lengths = lengths.at[source_of].add(-moved).at[sink].add(moved)
    members = jnp.searchsorted(jnp.cumsum(lengths), jnp.arange(rows * top), side="right").astype(jnp.int32)
    listing = members.reshape(top, rows).T
    listing = listing[jax.random.permutation(jax.random.fold_in(own, 1), rows)]
    turn = jax.random.randint(jax.random.fold_in(own, 2), (rows, 1), 0, top)
    return jnp.take_along_axis(listing, (jnp.arange(top)[None, :] + turn) % top, axis=1)


def shares(number_of, total, reach, skew, full):
    portions = [(1 << 20) // math.isqrt(grade ** skew) + 1 for grade in range(1, number_of + 1)]
    largest = reach if full else min(reach, max(-(-total // number_of), total * portions[0] // sum(portions)))
    least = 1 if total - largest >= number_of - 1 else 0
    given, rest = [largest] + [least] * (number_of - 1), total - largest - least * (number_of - 1)
    while rest > 0:
        candidates = [i for i in range(1, number_of) if given[i] < largest] or [i for i in range(1, number_of) if given[i] < reach]
        pool, left = sum([portions[i] for i in candidates]), rest
        for i in candidates:
            more = min(reach - given[i], max(1, left * portions[i] // pool), rest)
            given[i] = given[i] + more
            rest = rest - more
    return np.array(given)


def noise(own_key, dims, deviation, most, pieces=(), kind=jnp.bfloat16):
    level = level_of(own_key, dims, pieces, -0.22, 0.18) if pieces else 1.0
    values = jax.random.normal(own_key, dims, jnp.float32) * deviation * level
    return jnp.minimum(jnp.maximum(values, -most), most).astype(kind)


def setup_inputs(seed: int = 0) -> dict:
    splits = jax.random.split(jax.random.key(seed), 8)
    amplitudes = noise(splits[0], (PAIRS, NPNO, NPNO), 1.0, 6.0, ((0, 16),))
    pno_coef = noise(splits[1], (PAIRS, NPAO, NPNO), ((LINKS * NPNO * NPNO) ** -0.125 * NPAO ** -0.25), 0.75, ((0, 16),))
    ladder_ints = noise(splits[2], (NAUXF, NPNO, NPNO), ((NAUXF * NPNO * NPNO) ** -0.25), 0.3125, ((0, 2),))
    coulomb_ints = noise(splits[3], (PAIRS, NPNO, NPNO), 1.0, 6.0, ((0, 32),))
    pno_energy = jnp.clip(jnp.exp(math.log(3.0) - 2.3025851 * jax.random.uniform(splits[4], (PAIRS, NPNO), jnp.float32) ** level_of(splits[4], (PAIRS, NPNO), ((0, 32),), -0.2, 0.2)), 0.3, 3.0)
    link_owner_keys = jax.random.split(jax.random.fold_in(splits[5], 1), LINK_ROWS // SLOTS)
    link_owner_turns = jax.random.permutation(jax.random.fold_in(splits[5], 3), LINK_ROWS // SLOTS)
    link_owner = jax.vmap(lambda own, number: routed_block(jax.random.fold_in(splits[5], 2), own, number, SLOTS, N_PAIRS, 1, CAP, 2))(link_owner_keys, link_owner_turns).reshape((LINK_ROWS, 1))
    link_local = place_ends(jax.random.randint(splits[6], (LINK_ROWS, 1), 0, PAIR_DEV), jax.random.fold_in(splits[6], 1), 0, PAIR_DEV - 1).astype(jnp.int32)
    return {"amplitudes": amplitudes, "pno_coef": pno_coef, "ladder_ints": ladder_ints, "coulomb_ints": coulomb_ints, "pno_energy": pno_energy, "link_owner": link_owner, "link_local": link_local}


def reference(amplitudes, pno_coef, ladder_ints, coulomb_ints, pno_energy, link_owner, link_local):
    target = (link_owner[:, 0] * PAIR_DEV + link_local[:, 0]).astype(jnp.int32)
    target = jnp.transpose(target.reshape(N_PAIRS, N_AUX, PAIR_DEV, LPS), (0, 2, 1, 3)).reshape(PAIRS, LINKS)
    blocks = ladder_ints.astype(jnp.float32)

    def one_pair(inputs):
        coef_p, amp_p, targets = inputs
        coef_q = pno_coef[targets].astype(jnp.float32)
        amp_q = amplitudes[targets].astype(jnp.float32)
        intersection = jnp.einsum("ac,lad->lcd", coef_p.astype(jnp.float32), coef_q).astype(jnp.bfloat16)
        intersection = lax.optimization_barrier(intersection).astype(jnp.float32)
        halfway = jnp.einsum("lcd,lde->lce", intersection, amp_q).astype(jnp.bfloat16)
        halfway = lax.optimization_barrier(halfway).astype(jnp.float32)
        linked = jnp.einsum("lce,lfe->cf", halfway, intersection)
        ladder_half = jnp.einsum("qcd,de->qce", blocks, amp_p.astype(jnp.float32)).astype(jnp.bfloat16)
        ladder_half = lax.optimization_barrier(ladder_half).astype(jnp.float32)
        ladder = jnp.einsum("qce,qfe->cf", ladder_half, blocks)
        return linked + ladder

    pair_sums = lax.map(one_pair, (pno_coef, amplitudes, target))
    residual = coulomb_ints.astype(jnp.float32) + pair_sums
    denominator = pno_energy[:, :, None] + pno_energy[:, None, :]
    return amplitudes.astype(jnp.float32) - residual / denominator
```

```python
import functools

import jax
import jax.numpy as jnp
from jax import lax
from jax.experimental import pallas as pl
from jax.experimental.pallas import tpu as pltpu
from jax.sharding import PartitionSpec as P

MESH = pl.DeviceIdType.MESH
BF = jnp.bfloat16
F32 = jnp.float32
LANES = 128
CHUNK = 4


def dot(x, y, dims=((1,), (0,))):
    return lax.dot_general(x, y, (dims, ((), ())), preferred_element_type=F32)


def link_counts(link_owner, link_local, pair_dev, pairs):
    target = (link_owner * pair_dev + link_local).reshape(pair_dev, -1, 1)
    hit = target == jnp.arange(pairs, dtype=jnp.int32)[None, None, :]
    return jnp.sum(hit.astype(F32), axis=1)


def fused_kernel(
    n, cuts, amp, coef, ints, counts, coulomb, energy, out,
    msg_out, msg_in, sum_out, sum_in, shuffle, acc, other_counts, other_acc,
    msg_send, msg_recv, sum_send, sum_recv, aux_send, aux_recv,
):
    g, a = lax.axis_index("pairs"), lax.axis_index("aux")
    other = 1 - a
    pair_dev, width, _ = amp.shape
    pao = coef.shape[1]
    rows = pao // 2
    band = rows // n
    tiles = 2 * band
    own = coulomb.shape[0]
    count_tiles = counts.shape[0]

    def partner(k):
        return lax.rem(g + lax.rem(k + n // 2 - 1, n - 1) + 1, n)

    barrier = pltpu.get_barrier_semaphore()

    def greet(k, _):
        pl.semaphore_signal(barrier, inc=1, device_id=(partner(k), a), device_id_type=MESH)
        return 0

    lax.fori_loop(1, n, greet, 0)
    pl.semaphore_signal(barrier, inc=1, device_id=(g, other), device_id_type=MESH)

    mine = pl.ds(pl.multiple_of(a * rows, rows), rows)

    def backproject(q, _):
        half = dot(coef[q, mine, :], amp[q]).astype(BF)
        m = dot(half, coef[q], ((1,), (1,)))
        for side in range(2):
            start = pl.multiple_of((q * 2 + side) * rows, rows)
            shuffle[pl.ds(start, rows), :] = m[:, side * LANES:(side + 1) * LANES]
        return 0

    lax.fori_loop(0, pair_dev, backproject, 0)

    pl.semaphore_wait(barrier, n)
    swap = pltpu.make_async_remote_copy(
        src_ref=counts, dst_ref=other_counts, send_sem=aux_send.at[0], recv_sem=aux_recv.at[0],
        device_id=(g, other), device_id_type=MESH,
    )
    swap.start()
    swap.wait()
    all_counts = counts[...] + other_counts[...]

    def pack(h):
        for side in range(2):
            for r in range(band):
                tile = shuffle[pl.ds(side * rows + h * band + r, pair_dev, stride=2 * rows), :]
                msg_out[h, side * band + r] = tile.astype(BF)
        msg_out[h, tiles:tiles + count_tiles] = all_counts

    def message(h, slot):
        return pltpu.make_async_remote_copy(
            src_ref=msg_out.at[h], dst_ref=msg_in.at[slot], send_sem=msg_send.at[h],
            recv_sem=msg_recv.at[slot], device_id=(h, a), device_id_type=MESH,
        )

    def sums(h, slot):
        return pltpu.make_async_remote_copy(
            src_ref=sum_out.at[h], dst_ref=sum_in.at[slot], send_sem=sum_send.at[h],
            recv_sem=sum_recv.at[slot], device_id=(h, a), device_id_type=MESH,
        )

    def ship(k, _):
        h = partner(k)
        pack(h)
        message(h, g).start()
        return 0

    lax.fori_loop(1, n, ship, 0)
    pack(g)
    msg_in[g] = msg_out[g]

    acc[...] = jnp.zeros_like(acc)

    def ladder(step, _):
        block = ints[pl.ds(step * CHUNK, CHUNK)]
        stacked = block.reshape(CHUNK * width, width)
        wide = jnp.concatenate([block[j] for j in range(CHUNK)], axis=1)
        for pp in range(pair_dev // 2):
            two = amp[2 * pp:2 * pp + 2].reshape(2 * width, width)
            half = dot(two, stacked, ((1,), (1,))).astype(BF)
            turned = jnp.concatenate(
                [
                    jnp.concatenate(
                        [half[i * width:(i + 1) * width, j * width:(j + 1) * width] for i in range(2)],
                        axis=1,
                    )
                    for j in range(CHUNK)
                ],
                axis=0,
            )
            acc[pp] += dot(wide, turned)
        return 0

    lax.fori_loop(0, cuts[0], ladder, 0)

    def take_message(k, _):
        message(partner(k), partner(k)).wait_recv()
        return 0

    lax.fori_loop(1, n, take_message, 0)

    matrix = jnp.concatenate(
        [msg_in[:, tiles + j].reshape(n * pair_dev, LANES) for j in range(count_tiles)], axis=1
    )
    for t in range(0, tiles, 2):
        both = jnp.concatenate(
            [msg_in[:, t + j].reshape(n * pair_dev, LANES) for j in range(2)], axis=1
        )
        total = dot(matrix, both).astype(BF)
        for j in range(2):
            sum_out[:, t + j] = total[:, j * LANES:(j + 1) * LANES].reshape(n, pair_dev, LANES)

    def ship_sums(k, _):
        sums(partner(k), g).start()
        return 0

    lax.fori_loop(1, n, ship_sums, 0)
    sum_in[g] = sum_out[g]

    lax.fori_loop(cuts[0], cuts[1], ladder, 0)

    def take_sums(k, _):
        sums(partner(k), partner(k)).wait_recv()
        return 0

    lax.fori_loop(1, n, take_sums, 0)

    def spread(h, _):
        for side in range(2):
            start = pl.multiple_of((side * n + h) * band * pair_dev, band * pair_dev)
            part = sum_in[h, side * band:(side + 1) * band]
            shuffle[pl.ds(start, band * pair_dev), :] = part.reshape(band * pair_dev, LANES).astype(F32)
        return 0

    lax.fori_loop(0, n, spread, 0)

    def project(pp, _):
        found = []
        for i in range(2):
            p = 2 * pp + i
            s = jnp.concatenate(
                [
                    shuffle[pl.ds(side * rows * pair_dev + p, rows, stride=pair_dev), :].astype(BF)
                    for side in range(2)
                ],
                axis=1,
            )
            y = dot(s, coef[p]).astype(BF)
            found.append(dot(coef[p, mine, :], y, ((0,), (0,))))
        acc[pp] += jnp.concatenate(found, axis=1)
        return 0

    few = own // 2
    lax.fori_loop(other * few, other * few + few, project, 0)
    trade = pltpu.make_async_remote_copy(
        src_ref=acc.at[pl.ds(other * few, few)], dst_ref=other_acc, send_sem=aux_send.at[1],
        recv_sem=aux_recv.at[1], device_id=(g, other), device_id_type=MESH,
    )
    trade.start()
    lax.fori_loop(a * few, a * few + few, project, 0)
    trade.wait()

    for i in range(own):
        lanes = slice((i % 2) * width, (i % 2 + 1) * width)
        reduced = acc[a * few + i // 2, :, lanes] + other_acc[i // 2, :, lanes]
        residual = coulomb[i].astype(F32) + reduced
        line = jnp.broadcast_to(energy[i:i + 1, :], (width, width))
        out[i] = amp[a * own + i].astype(F32) - residual / (line + line.T)

    def finish(k, _):
        message(partner(k), g).wait_send()
        sums(partner(k), g).wait_send()
        return 0

    lax.fori_loop(1, n, finish, 0)


def fused(amplitudes, pno_coef, ladder_ints, coulomb_ints, pno_energy, link_owner, link_local):
    n = lax.axis_size("pairs")
    pair_dev, width, _ = amplitudes.shape
    pao = pno_coef.shape[1]
    pairs = n * pair_dev
    counts = link_counts(link_owner, link_local, pair_dev, pairs).astype(BF)
    count_tiles = pairs // LANES
    counts = jnp.swapaxes(counts.reshape(pair_dev, count_tiles, LANES), 0, 1)
    band = pao // 2 // n
    tiles = 2 * band
    own = coulomb_ints.shape[0]
    steps = ladder_ints.shape[0] // CHUNK
    return pl.pallas_call(
        functools.partial(fused_kernel, n, (steps // 2, steps)),
        out_shape=jax.ShapeDtypeStruct(coulomb_ints.shape, F32),
        in_specs=[pl.BlockSpec(memory_space=pltpu.VMEM)] * 6,
        out_specs=pl.BlockSpec(memory_space=pltpu.VMEM),
        scratch_shapes=[
            pltpu.VMEM((n, tiles + count_tiles, pair_dev, LANES), BF),
            pltpu.VMEM((n, tiles + count_tiles, pair_dev, LANES), BF),
            pltpu.VMEM((n, tiles, pair_dev, LANES), BF),
            pltpu.VMEM((n, tiles, pair_dev, LANES), BF),
            pltpu.VMEM((pair_dev * pao, LANES), F32),
            pltpu.VMEM((pair_dev // 2, width, 2 * width), F32),
            pltpu.VMEM(counts.shape, BF),
            pltpu.VMEM((own // 2, width, 2 * width), F32),
            pltpu.SemaphoreType.DMA((n,)),
            pltpu.SemaphoreType.DMA((n,)),
            pltpu.SemaphoreType.DMA((n,)),
            pltpu.SemaphoreType.DMA((n,)),
            pltpu.SemaphoreType.DMA((2,)),
            pltpu.SemaphoreType.DMA((2,)),
        ],
        compiler_params=pltpu.CompilerParams(
            collective_id=0, has_side_effects=True, vmem_limit_bytes=48 * 2**20
        ),
    )(amplitudes, pno_coef, ladder_ints, counts, coulomb_ints, pno_energy)


def general(amplitudes, pno_coef, ladder_ints, coulomb_ints, pno_energy, link_owner, link_local):
    groups, parts = lax.axis_size("pairs"), lax.axis_size("aux")
    devices = groups * parts
    pair_dev, width, _ = amplitudes.shape
    pao = pno_coef.shape[1]
    own = coulomb_ints.shape[0]
    first = lax.axis_index("aux") * own
    both = ("pairs", "aux")
    counts = link_counts(link_owner, link_local, pair_dev, groups * pair_dev)
    matrix = lax.all_gather(lax.psum(counts, "aux"), "pairs", axis=0, tiled=True).astype(BF)
    amp = lax.dynamic_slice_in_dim(amplitudes, first, own, 0)
    coef = lax.dynamic_slice_in_dim(pno_coef, first, own, 0)
    half = jnp.einsum("qac,qcd->qad", coef, amp, preferred_element_type=F32).astype(BF)
    back = jnp.einsum("qad,qbd->qab", half, coef, preferred_element_type=F32).astype(BF)
    back = jnp.swapaxes(back.reshape(own, devices, -1), 0, 1)
    back = lax.all_to_all(back, both, split_axis=0, concat_axis=0, tiled=True)
    total = dot(matrix, back.reshape(devices * own, -1)).astype(BF)
    total = lax.all_to_all(
        total.reshape(devices, own, -1), both, split_axis=0, concat_axis=0, tiled=True
    )
    total = jnp.swapaxes(total, 0, 1).reshape(own, pao, pao)
    near = jnp.einsum("pab,pbd->pad", total, coef, preferred_element_type=F32).astype(BF)
    linked = jnp.einsum("pac,pad->pcd", coef, near, preferred_element_type=F32)

    def ladder_terms(amp_p):
        ladder_half = jnp.einsum(
            "qcd,de->qce", ladder_ints, amp_p, preferred_element_type=F32
        ).astype(BF)
        return jnp.einsum("qce,qfe->cf", ladder_half, ladder_ints, preferred_element_type=F32)

    ladder = lax.psum_scatter(
        lax.map(ladder_terms, amplitudes), "aux", scatter_dimension=0, tiled=True
    )
    residual = coulomb_ints.astype(F32) + ladder + linked
    denominator = pno_energy[:, :, None] + pno_energy[:, None, :]
    return amp.astype(F32) - residual / denominator


def local(*arrays):
    amplitudes, pno_coef, ladder_ints = arrays[:3]
    n = lax.axis_size("pairs")
    fits = (
        lax.axis_size("aux") == 2
        and amplitudes.shape[1] == LANES
        and pno_coef.shape[1] == 2 * LANES
        and amplitudes.shape[0] == 16
        and LANES % (8 * n) == 0
        and n * 16 % LANES == 0
        and ladder_ints.shape[0] % CHUNK == 0
    )
    return fused(*arrays) if fits else general(*arrays)


def solution(mesh):
    in_specs = (
        P("pairs", None, None),
        P("pairs", None, None),
        P("aux", None, None),
        P(("pairs", "aux"), None, None),
        P(("pairs", "aux"), None),
        P(("pairs", "aux"), None),
        P(("pairs", "aux"), None),
    )
    out_specs = P(("pairs", "aux"), None, None)
    return jax.shard_map(local, mesh=mesh, in_specs=in_specs, out_specs=out_specs, check_vma=False)
```

```python
import functools

import jax
import jax.numpy as jnp
from jax import lax
from jax.experimental import pallas as pl
from jax.experimental.pallas import tpu as pltpu
from jax.sharding import PartitionSpec as P

MESH = pl.DeviceIdType.MESH
BF = jnp.bfloat16
F32 = jnp.float32
LANES = 128
CHUNK = 4


def dot(x, y, dims=((1,), (0,))):
    return lax.dot_general(x, y, (dims, ((), ())), preferred_element_type=F32)


def link_counts(link_owner, link_local, pair_dev, pairs):
    target = (link_owner * pair_dev + link_local).reshape(pair_dev, -1, 1)
    hit = target == jnp.arange(pairs, dtype=jnp.int32)[None, None, :]
    return jnp.sum(hit.astype(F32), axis=1)


def fused_kernel(
    n, cuts, amp_hbm, coef_hbm, ints_hbm, counts_hbm, coulomb_hbm, energy_hbm, out,
    amp, coef, ints, counts, coulomb, energy,
    msg_out, msg_in, sum_out, sum_in, shuffle, acc, other_counts, other_acc,
    load, msg_send, msg_recv, sum_send, sum_recv, aux_send, aux_recv,
):
    g, a = lax.axis_index("pairs"), lax.axis_index("aux")
    other = 1 - a
    pair_dev, width, _ = amp.shape
    pao = coef.shape[1]
    rows = pao // 2
    band = rows // n
    own = coulomb.shape[0]
    count_tiles = counts.shape[0]
    spans = ((0, count_tiles + band), (count_tiles + band, band))

    loads = [
        pltpu.make_async_copy(src, dst, load.at[i])
        for i, (src, dst) in enumerate(
            (
                (amp_hbm, amp), (coef_hbm, coef), (counts_hbm, counts),
                (ints_hbm, ints), (coulomb_hbm, coulomb), (energy_hbm, energy),
            )
        )
    ]
    for copy in loads:
        copy.start()

    def partner(k):
        return lax.rem(g + lax.rem(k + n // 2 - 1, n - 1) + 1, n)

    barrier = pltpu.get_barrier_semaphore()

    def greet(k, _):
        pl.semaphore_signal(barrier, inc=1, device_id=(partner(k), a), device_id_type=MESH)
        return 0

    lax.fori_loop(1, n, greet, 0)
    pl.semaphore_signal(barrier, inc=1, device_id=(g, other), device_id_type=MESH)
    for copy in loads[:3]:
        copy.wait()

    mine = pl.ds(pl.multiple_of(a * rows, rows), rows)

    def backproject(q, _):
        half = dot(coef[q, mine, :], amp[q]).astype(BF)
        m = dot(half, coef[q], ((1,), (1,)))
        for side in range(2):
            start = pl.multiple_of((q * 2 + side) * rows, rows)
            shuffle[pl.ds(start, rows), :] = m[:, side * LANES:(side + 1) * LANES]
        return 0

    lax.fori_loop(0, pair_dev // 2, backproject, 0, unroll=4)
    pl.semaphore_wait(barrier, n)
    swap = pltpu.make_async_remote_copy(
        src_ref=counts, dst_ref=other_counts, send_sem=aux_send.at[0], recv_sem=aux_recv.at[0],
        device_id=(g, other), device_id_type=MESH,
    )
    swap.start()
    lax.fori_loop(pair_dev // 2, pair_dev, backproject, 0, unroll=4)
    swap.wait()
    all_counts = counts[...] + other_counts[...]

    def pack(h, side):
        for r in range(band):
            tile = shuffle[pl.ds(side * rows + h * band + r, pair_dev, stride=2 * rows), :]
            msg_out[h, count_tiles + side * band + r] = tile.astype(BF)
        if side == 0:
            msg_out[h, :count_tiles] = all_counts

    def message(side, h, slot):
        part = pl.ds(*spans[side])
        return pltpu.make_async_remote_copy(
            src_ref=msg_out.at[h, part], dst_ref=msg_in.at[slot, part],
            send_sem=msg_send.at[side, h], recv_sem=msg_recv.at[side, slot],
            device_id=(h, a), device_id_type=MESH,
        )

    def sums(side, h, slot):
        part = pl.ds(side * band, band)
        return pltpu.make_async_remote_copy(
            src_ref=sum_out.at[h, part], dst_ref=sum_in.at[slot, part],
            send_sem=sum_send.at[side, h], recv_sem=sum_recv.at[side, slot],
            device_id=(h, a), device_id_type=MESH,
        )

    def ship(side, k, _):
        h = partner(k)
        pack(h, side)
        message(side, h, g).start()
        return 0

    for side in range(2):
        lax.fori_loop(1, n, functools.partial(ship, side), 0)
    for side in range(2):
        pack(g, side)
    msg_in[g] = msg_out[g]

    acc[...] = jnp.zeros_like(acc)
    for copy in loads[3:]:
        copy.wait()

    def ladder(step, _):
        block = ints[pl.ds(step * CHUNK, CHUNK)]
        flipped = jnp.concatenate([block[j].T for j in range(CHUNK)], axis=1)
        wide = jnp.concatenate([block[j] for j in range(CHUNK)], axis=1)

        def first(pp):
            two = amp[2 * pp:2 * pp + 2].reshape(2 * width, width)
            return dot(two, flipped).astype(BF)

        half = first(0)
        for pp in range(pair_dev // 2):
            coming = first(pp + 1) if pp + 1 < pair_dev // 2 else None
            turned = jnp.concatenate(
                [
                    jnp.concatenate(
                        [half[i * width:(i + 1) * width, j * width:(j + 1) * width] for i in range(2)],
                        axis=1,
                    )
                    for j in range(CHUNK)
                ],
                axis=0,
            )
            acc[pp] += dot(wide, turned)
            half = coming
        return 0

    def take_messages(side):
        def take(k, _):
            message(side, partner(k), partner(k)).wait_recv()
            return 0

        lax.fori_loop(1, n, take, 0)

    def add_up(side):
        matrix = jnp.concatenate(
            [msg_in[:, j].reshape(n * pair_dev, LANES) for j in range(count_tiles)], axis=1
        )
        for t in range(side * band, (side + 1) * band, 2):
            both = jnp.concatenate(
                [msg_in[:, count_tiles + t + j].reshape(n * pair_dev, LANES) for j in range(2)],
                axis=1,
            )
            total = dot(matrix, both).astype(BF)
            for j in range(2):
                sum_out[:, t + j] = total[:, j * LANES:(j + 1) * LANES].reshape(n, pair_dev, LANES)

        def ship_sums(k, _):
            sums(side, partner(k), g).start()
            return 0

        lax.fori_loop(1, n, ship_sums, 0)

    start = 0
    for side in range(2):
        lax.fori_loop(start, cuts[side], ladder, 0)
        start = cuts[side]
        take_messages(side)
        add_up(side)
    sum_in[g] = sum_out[g]
    lax.fori_loop(start, cuts[2], ladder, 0)

    for side in range(2):
        def take_sums(k, _):
            sums(side, partner(k), partner(k)).wait_recv()
            return 0

        lax.fori_loop(1, n, take_sums, 0)

        def spread(h, _):
            place = pl.multiple_of((side * n + h) * band * pair_dev, band * pair_dev)
            part = sum_in[h, side * band:(side + 1) * band]
            shuffle[pl.ds(place, band * pair_dev), :] = part.reshape(band * pair_dev, LANES).astype(F32)
            return 0

        lax.fori_loop(0, n, spread, 0, unroll=4)

    def project(pp):
        found = []
        for i in range(2):
            p = 2 * pp + i
            s = jnp.concatenate(
                [
                    shuffle[pl.ds(side * rows * pair_dev + p, rows, stride=pair_dev), :].astype(BF)
                    for side in range(2)
                ],
                axis=1,
            )
            y = dot(s, coef[p]).astype(BF)
            found.append(dot(coef[p, mine, :], y, ((0,), (0,))))
        acc[pp] += jnp.concatenate(found, axis=1)

    few = own // 2
    for j in range(few):
        project(other * few + j)
    trade = pltpu.make_async_remote_copy(
        src_ref=acc.at[pl.ds(other * few, few)], dst_ref=other_acc, send_sem=aux_send.at[1],
        recv_sem=aux_recv.at[1], device_id=(g, other), device_id_type=MESH,
    )
    trade.start()
    for j in range(few):
        project(a * few + j)
    trade.wait()

    for i in range(own):
        lanes = slice((i % 2) * width, (i % 2 + 1) * width)
        reduced = acc[a * few + i // 2, :, lanes] + other_acc[i // 2, :, lanes]
        residual = coulomb[i].astype(F32) + reduced
        line = jnp.broadcast_to(energy[i:i + 1, :], (width, width))
        out[i] = amp[a * own + i].astype(F32) - residual / (line + line.T)

    for side in range(2):
        def finish(k, _):
            message(side, partner(k), g).wait_send()
            sums(side, partner(k), g).wait_send()
            return 0

        lax.fori_loop(1, n, finish, 0)


def fused(amplitudes, pno_coef, ladder_ints, coulomb_ints, pno_energy, link_owner, link_local):
    n = lax.axis_size("pairs")
    pair_dev, width, _ = amplitudes.shape
    pao = pno_coef.shape[1]
    pairs = n * pair_dev
    counts = link_counts(link_owner, link_local, pair_dev, pairs).astype(BF)
    count_tiles = pairs // LANES
    counts = jnp.swapaxes(counts.reshape(pair_dev, count_tiles, LANES), 0, 1)
    band = pao // 2 // n
    tiles = 2 * band
    own = coulomb_ints.shape[0]
    steps = ladder_ints.shape[0] // CHUNK
    operands = (amplitudes, pno_coef, ladder_ints, counts, coulomb_ints, pno_energy)
    return pl.pallas_call(
        functools.partial(fused_kernel, n, (steps // 4, steps // 2, steps)),
        out_shape=jax.ShapeDtypeStruct(coulomb_ints.shape, F32),
        in_specs=[pl.BlockSpec(memory_space=pl.ANY)] * 6,
        out_specs=pl.BlockSpec(memory_space=pltpu.VMEM),
        scratch_shapes=[
            *(pltpu.VMEM(x.shape, x.dtype) for x in operands),
            pltpu.VMEM((n, tiles + count_tiles, pair_dev, LANES), BF),
            pltpu.VMEM((n, tiles + count_tiles, pair_dev, LANES), BF),
            pltpu.VMEM((n, tiles, pair_dev, LANES), BF),
            pltpu.VMEM((n, tiles, pair_dev, LANES), BF),
            pltpu.VMEM((pair_dev * pao, LANES), F32),
            pltpu.VMEM((pair_dev // 2, width, 2 * width), F32),
            pltpu.VMEM(counts.shape, BF),
            pltpu.VMEM((own // 2, width, 2 * width), F32),
            pltpu.SemaphoreType.DMA((len(operands),)),
            pltpu.SemaphoreType.DMA((2, n)),
            pltpu.SemaphoreType.DMA((2, n)),
            pltpu.SemaphoreType.DMA((2, n)),
            pltpu.SemaphoreType.DMA((2, n)),
            pltpu.SemaphoreType.DMA((2,)),
            pltpu.SemaphoreType.DMA((2,)),
        ],
        compiler_params=pltpu.CompilerParams(
            collective_id=0, has_side_effects=True, vmem_limit_bytes=62 * 2**20
        ),
    )(*operands)


def general(amplitudes, pno_coef, ladder_ints, coulomb_ints, pno_energy, link_owner, link_local):
    groups, parts = lax.axis_size("pairs"), lax.axis_size("aux")
    devices = groups * parts
    pair_dev, width, _ = amplitudes.shape
    pao = pno_coef.shape[1]
    own = coulomb_ints.shape[0]
    first = lax.axis_index("aux") * own
    both = ("pairs", "aux")
    counts = link_counts(link_owner, link_local, pair_dev, groups * pair_dev)
    matrix = lax.all_gather(lax.psum(counts, "aux"), "pairs", axis=0, tiled=True).astype(BF)
    amp = lax.dynamic_slice_in_dim(amplitudes, first, own, 0)
    coef = lax.dynamic_slice_in_dim(pno_coef, first, own, 0)
    half = jnp.einsum("qac,qcd->qad", coef, amp, preferred_element_type=F32).astype(BF)
    back = jnp.einsum("qad,qbd->qab", half, coef, preferred_element_type=F32).astype(BF)
    back = jnp.swapaxes(back.reshape(own, devices, -1), 0, 1)
    back = lax.all_to_all(back, both, split_axis=0, concat_axis=0, tiled=True)
    total = dot(matrix, back.reshape(devices * own, -1)).astype(BF)
    total = lax.all_to_all(
        total.reshape(devices, own, -1), both, split_axis=0, concat_axis=0, tiled=True
    )
    total = jnp.swapaxes(total, 0, 1).reshape(own, pao, pao)
    near = jnp.einsum("pab,pbd->pad", total, coef, preferred_element_type=F32).astype(BF)
    linked = jnp.einsum("pac,pad->pcd", coef, near, preferred_element_type=F32)

    def ladder_terms(amp_p):
        ladder_half = jnp.einsum(
            "qcd,de->qce", ladder_ints, amp_p, preferred_element_type=F32
        ).astype(BF)
        return jnp.einsum("qce,qfe->cf", ladder_half, ladder_ints, preferred_element_type=F32)

    ladder = lax.psum_scatter(
        lax.map(ladder_terms, amplitudes), "aux", scatter_dimension=0, tiled=True
    )
    residual = coulomb_ints.astype(F32) + ladder + linked
    denominator = pno_energy[:, :, None] + pno_energy[:, None, :]
    return amp.astype(F32) - residual / denominator


def local(*arrays):
    amplitudes, pno_coef, ladder_ints = arrays[:3]
    n = lax.axis_size("pairs")
    fits = (
        lax.axis_size("aux") == 2
        and amplitudes.shape[1] == LANES
        and pno_coef.shape[1] == 2 * LANES
        and amplitudes.shape[0] == 16
        and LANES % (8 * n) == 0
        and n * 16 % LANES == 0
        and ladder_ints.shape[0] % CHUNK == 0
    )
    return fused(*arrays) if fits else general(*arrays)


def solution(mesh):
    in_specs = (
        P("pairs", None, None),
        P("pairs", None, None),
        P("aux", None, None),
        P(("pairs", "aux"), None, None),
        P(("pairs", "aux"), None),
        P(("pairs", "aux"), None),
        P(("pairs", "aux"), None),
    )
    out_specs = P(("pairs", "aux"), None, None)
    return jax.shard_map(local, mesh=mesh, in_specs=in_specs, out_specs=out_specs, check_vma=False)
```

```python
import functools

import jax
import jax.numpy as jnp
from jax import lax
from jax.experimental import pallas as pl
from jax.experimental.pallas import tpu as pltpu
from jax.sharding import PartitionSpec as P

MESH = pl.DeviceIdType.MESH
BF = jnp.bfloat16
F32 = jnp.float32
LANES = 128
CHUNK = 4


def dot(x, y, dims=((1,), (0,))):
    return lax.dot_general(x, y, (dims, ((), ())), preferred_element_type=F32)


def link_counts(link_owner, link_local, pair_dev, pairs):
    target = (link_owner * pair_dev + link_local).reshape(pair_dev, -1, 1)
    hit = target == jnp.arange(pairs, dtype=jnp.int32)[None, None, :]
    return jnp.sum(hit.astype(F32), axis=1)


def fused_kernel(
    n, cuts, amp_hbm, coef_hbm, ints_hbm, owner_hbm, local_hbm, coulomb_hbm, energy_hbm, out,
    amp, coef, ints, owner, local_index, coulomb, energy, counts,
    msg_out, msg_in, sum_out, sum_in, shuffle, acc, other_counts, other_acc,
    load, msg_send, msg_recv, sum_send, sum_recv, aux_send, aux_recv,
):
    g, a = lax.axis_index("pairs"), lax.axis_index("aux")
    other = 1 - a
    pair_dev, width, _ = amp.shape
    pao = coef.shape[1]
    rows = pao // 2
    band = rows // n
    own = coulomb.shape[0]
    count_tiles = counts.shape[0]
    spans = ((0, count_tiles + band), (count_tiles + band, band))

    loads = [
        pltpu.make_async_copy(src, dst, load.at[i])
        for i, (src, dst) in enumerate(
            (
                (amp_hbm, amp), (coef_hbm, coef), (owner_hbm, owner), (local_hbm, local_index),
                (ints_hbm, ints), (coulomb_hbm, coulomb), (energy_hbm, energy),
            )
        )
    ]
    for copy in loads:
        copy.start()

    def partner(k):
        return lax.rem(g + lax.rem(k + n // 2 - 1, n - 1) + 1, n)

    barrier = pltpu.get_barrier_semaphore()

    def greet(k, _):
        pl.semaphore_signal(barrier, inc=1, device_id=(partner(k), a), device_id_type=MESH)
        return 0

    lax.fori_loop(1, n, greet, 0)
    pl.semaphore_signal(barrier, inc=1, device_id=(g, other), device_id_type=MESH)
    for copy in loads[:4]:
        copy.wait()

    mine = pl.ds(pl.multiple_of(a * rows, rows), rows)

    def backproject(q, _):
        half = dot(coef[q, mine, :], amp[q]).astype(BF)
        m = dot(half, coef[q], ((1,), (1,)))
        for side in range(2):
            start = pl.multiple_of((q * 2 + side) * rows, rows)
            shuffle[pl.ds(start, rows), :] = m[:, side * LANES:(side + 1) * LANES]
        return 0

    slots = owner.shape[1]
    per_pair = slots // pair_dev
    target = owner[...] * pair_dev + local_index[...]
    hit = lax.broadcasted_iota(jnp.int32, (n * pair_dev, slots), 0) == target
    first_slot = lax.broadcasted_iota(jnp.int32, (pair_dev, slots), 0) * per_pair
    slot = lax.broadcasted_iota(jnp.int32, (pair_dev, slots), 1)
    own_slot = (slot >= first_slot) & (slot < first_slot + per_pair)
    found = dot(
        jnp.where(own_slot, 1.0, 0.0).astype(BF), jnp.where(hit, 1.0, 0.0).astype(BF), ((1,), (1,))
    ).astype(BF)
    for j in range(count_tiles):
        counts[j] = found[:, j * LANES:(j + 1) * LANES]

    lax.fori_loop(0, pair_dev // 2, backproject, 0, unroll=4)
    pl.semaphore_wait(barrier, n)
    swap = pltpu.make_async_remote_copy(
        src_ref=counts, dst_ref=other_counts, send_sem=aux_send.at[0], recv_sem=aux_recv.at[0],
        device_id=(g, other), device_id_type=MESH,
    )
    swap.start()
    lax.fori_loop(pair_dev // 2, pair_dev, backproject, 0, unroll=4)
    swap.wait()
    all_counts = counts[...] + other_counts[...]

    def pack(h, side):
        for r in range(band):
            tile = shuffle[pl.ds(side * rows + h * band + r, pair_dev, stride=2 * rows), :]
            msg_out[h, count_tiles + side * band + r] = tile.astype(BF)
        if side == 0:
            msg_out[h, :count_tiles] = all_counts

    def message(side, h, slot):
        part = pl.ds(*spans[side])
        return pltpu.make_async_remote_copy(
            src_ref=msg_out.at[h, part], dst_ref=msg_in.at[slot, part],
            send_sem=msg_send.at[side, h], recv_sem=msg_recv.at[side, slot],
            device_id=(h, a), device_id_type=MESH,
        )

    def sums(side, h, slot):
        part = pl.ds(side * band, band)
        return pltpu.make_async_remote_copy(
            src_ref=sum_out.at[h, part], dst_ref=sum_in.at[slot, part],
            send_sem=sum_send.at[side, h], recv_sem=sum_recv.at[side, slot],
            device_id=(h, a), device_id_type=MESH,
        )

    def ship(side, k, _):
        h = partner(k)
        pack(h, side)
        message(side, h, g).start()
        return 0

    for side in range(2):
        lax.fori_loop(1, n, functools.partial(ship, side), 0)
    for side in range(2):
        pack(g, side)
    msg_in[g] = msg_out[g]

    acc[...] = jnp.zeros_like(acc)
    for copy in loads[4:]:
        copy.wait()

    def ladder(step, _):
        block = ints[pl.ds(step * CHUNK, CHUNK)]
        flipped = jnp.concatenate([block[j].T for j in range(CHUNK)], axis=1)
        wide = jnp.concatenate([block[j] for j in range(CHUNK)], axis=1)

        def first(quad):
            four = amp[4 * quad:4 * quad + 4].reshape(4 * width, width)
            return dot(four, flipped).astype(BF)

        half = first(0)
        for quad in range(pair_dev // 4):
            coming = first(quad + 1) if quad + 1 < pair_dev // 4 else None
            for pp in range(2):
                turned = jnp.concatenate(
                    [
                        jnp.concatenate(
                            [
                                half[i * width:(i + 1) * width, j * width:(j + 1) * width]
                                for i in (2 * pp, 2 * pp + 1)
                            ],
                            axis=1,
                        )
                        for j in range(CHUNK)
                    ],
                    axis=0,
                )
                acc[2 * quad + pp] += dot(wide, turned)
            half = coming
        return 0

    def take_messages(side):
        def take(k, _):
            message(side, partner(k), partner(k)).wait_recv()
            return 0

        lax.fori_loop(1, n, take, 0)

    def add_up(side):
        matrix = jnp.concatenate(
            [msg_in[:, j].reshape(n * pair_dev, LANES) for j in range(count_tiles)], axis=1
        )
        for t in range(side * band, (side + 1) * band, 2):
            both = jnp.concatenate(
                [msg_in[:, count_tiles + t + j].reshape(n * pair_dev, LANES) for j in range(2)],
                axis=1,
            )
            total = dot(matrix, both).astype(BF)
            for j in range(2):
                sum_out[:, t + j] = total[:, j * LANES:(j + 1) * LANES].reshape(n, pair_dev, LANES)

        def ship_sums(k, _):
            sums(side, partner(k), g).start()
            return 0

        lax.fori_loop(1, n, ship_sums, 0)

    start = 0
    for side in range(2):
        lax.fori_loop(start, cuts[side], ladder, 0)
        start = cuts[side]
        take_messages(side)
        add_up(side)
    sum_in[g] = sum_out[g]

    def receive_sums(side):
        def take_sums(k, _):
            sums(side, partner(k), partner(k)).wait_recv()
            return 0

        lax.fori_loop(1, n, take_sums, 0)

        def spread(h, _):
            place = pl.multiple_of((side * n + h) * band * pair_dev, band * pair_dev)
            part = sum_in[h, side * band:(side + 1) * band]
            shuffle[pl.ds(place, band * pair_dev), :] = part.reshape(band * pair_dev, LANES).astype(F32)
            return 0

        lax.fori_loop(0, n, spread, 0, unroll=4)

    def project(side, pp):
        found = []
        for i in range(2):
            p = 2 * pp + i
            s = shuffle[pl.ds(side * rows * pair_dev + p, rows, stride=pair_dev), :].astype(BF)
            y = dot(s, coef[p, side * LANES:(side + 1) * LANES, :]).astype(BF)
            found.append(dot(coef[p, mine, :], y, ((0,), (0,))))
        acc[pp] += jnp.concatenate(found, axis=1)

    lax.fori_loop(start, cuts[2], ladder, 0)
    receive_sums(0)
    for pp in range(pair_dev // 2):
        project(0, pp)
    lax.fori_loop(cuts[2], cuts[3], ladder, 0)
    receive_sums(1)

    few = own // 2
    for j in range(few):
        project(1, other * few + j)
    trade = pltpu.make_async_remote_copy(
        src_ref=acc.at[pl.ds(other * few, few)], dst_ref=other_acc, send_sem=aux_send.at[1],
        recv_sem=aux_recv.at[1], device_id=(g, other), device_id_type=MESH,
    )
    trade.start()
    for j in range(few):
        project(1, a * few + j)
    trade.wait()

    for i in range(own):
        lanes = slice((i % 2) * width, (i % 2 + 1) * width)
        reduced = acc[a * few + i // 2, :, lanes] + other_acc[i // 2, :, lanes]
        residual = coulomb[i].astype(F32) + reduced
        line = jnp.broadcast_to(energy[i:i + 1, :], (width, width))
        out[i] = amp[a * own + i].astype(F32) - residual / (line + line.T)

    for side in range(2):
        def finish(k, _):
            message(side, partner(k), g).wait_send()
            sums(side, partner(k), g).wait_send()
            return 0

        lax.fori_loop(1, n, finish, 0)


def fused(amplitudes, pno_coef, ladder_ints, coulomb_ints, pno_energy, link_owner, link_local):
    n = lax.axis_size("pairs")
    pair_dev, width, _ = amplitudes.shape
    pao = pno_coef.shape[1]
    pairs = n * pair_dev
    count_tiles = pairs // LANES
    band = pao // 2 // n
    tiles = 2 * band
    own = coulomb_ints.shape[0]
    steps = ladder_ints.shape[0] // CHUNK
    operands = (
        amplitudes, pno_coef, ladder_ints, link_owner.reshape(1, -1), link_local.reshape(1, -1),
        coulomb_ints, pno_energy,
    )
    return pl.pallas_call(
        functools.partial(fused_kernel, n, (steps // 4, steps // 2, 17 * steps // 20, steps)),
        out_shape=jax.ShapeDtypeStruct(coulomb_ints.shape, F32),
        in_specs=[pl.BlockSpec(memory_space=pl.ANY)] * len(operands),
        out_specs=pl.BlockSpec(memory_space=pltpu.VMEM),
        scratch_shapes=[
            *(pltpu.VMEM(x.shape, x.dtype) for x in operands),
            pltpu.VMEM((count_tiles, pair_dev, LANES), BF),
            pltpu.VMEM((n, tiles + count_tiles, pair_dev, LANES), BF),
            pltpu.VMEM((n, tiles + count_tiles, pair_dev, LANES), BF),
            pltpu.VMEM((n, tiles, pair_dev, LANES), BF),
            pltpu.VMEM((n, tiles, pair_dev, LANES), BF),
            pltpu.VMEM((pair_dev * pao, LANES), F32),
            pltpu.VMEM((pair_dev // 2, width, 2 * width), F32),
            pltpu.VMEM((count_tiles, pair_dev, LANES), BF),
            pltpu.VMEM((own // 2, width, 2 * width), F32),
            pltpu.SemaphoreType.DMA((len(operands),)),
            pltpu.SemaphoreType.DMA((2, n)),
            pltpu.SemaphoreType.DMA((2, n)),
            pltpu.SemaphoreType.DMA((2, n)),
            pltpu.SemaphoreType.DMA((2, n)),
            pltpu.SemaphoreType.DMA((2,)),
            pltpu.SemaphoreType.DMA((2,)),
        ],
        compiler_params=pltpu.CompilerParams(
            collective_id=0, has_side_effects=True, vmem_limit_bytes=60 * 2**20
        ),
    )(*operands)


def general(amplitudes, pno_coef, ladder_ints, coulomb_ints, pno_energy, link_owner, link_local):
    groups, parts = lax.axis_size("pairs"), lax.axis_size("aux")
    devices = groups * parts
    pair_dev, width, _ = amplitudes.shape
    pao = pno_coef.shape[1]
    own = coulomb_ints.shape[0]
    first = lax.axis_index("aux") * own
    both = ("pairs", "aux")
    counts = link_counts(link_owner, link_local, pair_dev, groups * pair_dev)
    matrix = lax.all_gather(lax.psum(counts, "aux"), "pairs", axis=0, tiled=True).astype(BF)
    amp = lax.dynamic_slice_in_dim(amplitudes, first, own, 0)
    coef = lax.dynamic_slice_in_dim(pno_coef, first, own, 0)
    half = jnp.einsum("qac,qcd->qad", coef, amp, preferred_element_type=F32).astype(BF)
    back = jnp.einsum("qad,qbd->qab", half, coef, preferred_element_type=F32).astype(BF)
    back = jnp.swapaxes(back.reshape(own, devices, -1), 0, 1)
    back = lax.all_to_all(back, both, split_axis=0, concat_axis=0, tiled=True)
    total = dot(matrix, back.reshape(devices * own, -1)).astype(BF)
    total = lax.all_to_all(
        total.reshape(devices, own, -1), both, split_axis=0, concat_axis=0, tiled=True
    )
    total = jnp.swapaxes(total, 0, 1).reshape(own, pao, pao)
    near = jnp.einsum("pab,pbd->pad", total, coef, preferred_element_type=F32).astype(BF)
    linked = jnp.einsum("pac,pad->pcd", coef, near, preferred_element_type=F32)

    def ladder_terms(amp_p):
        ladder_half = jnp.einsum(
            "qcd,de->qce", ladder_ints, amp_p, preferred_element_type=F32
        ).astype(BF)
        return jnp.einsum("qce,qfe->cf", ladder_half, ladder_ints, preferred_element_type=F32)

    ladder = lax.psum_scatter(
        lax.map(ladder_terms, amplitudes), "aux", scatter_dimension=0, tiled=True
    )
    residual = coulomb_ints.astype(F32) + ladder + linked
    denominator = pno_energy[:, :, None] + pno_energy[:, None, :]
    return amp.astype(F32) - residual / denominator


def local(*arrays):
    amplitudes, pno_coef, ladder_ints = arrays[:3]
    n = lax.axis_size("pairs")
    fits = (
        lax.axis_size("aux") == 2
        and amplitudes.shape[1] == LANES
        and pno_coef.shape[1] == 2 * LANES
        and amplitudes.shape[0] == 16
        and LANES % (8 * n) == 0
        and n * 16 % LANES == 0
        and ladder_ints.shape[0] % CHUNK == 0
    )
    return fused(*arrays) if fits else general(*arrays)


def solution(mesh):
    in_specs = (
        P("pairs", None, None),
        P("pairs", None, None),
        P("aux", None, None),
        P(("pairs", "aux"), None, None),
        P(("pairs", "aux"), None),
        P(("pairs", "aux"), None),
        P(("pairs", "aux"), None),
    )
    out_specs = P(("pairs", "aux"), None, None)
    return jax.shard_map(local, mesh=mesh, in_specs=in_specs, out_specs=out_specs, check_vma=False)
```

```python
import functools

import jax
import jax.numpy as jnp
from jax import lax
from jax.experimental import pallas as pl
from jax.experimental.pallas import tpu as pltpu
from jax.sharding import PartitionSpec as P

MESH = pl.DeviceIdType.MESH
BF = jnp.bfloat16
F32 = jnp.float32
LANES = 128
CHUNK = 8
BLOCK = 8


def dot(x, y, dims=((1,), (0,))):
    return lax.dot_general(x, y, (dims, ((), ())), preferred_element_type=F32)


def link_counts(link_owner, link_local, pair_dev, pairs):
    target = (link_owner * pair_dev + link_local).reshape(pair_dev, -1, 1)
    hit = target == jnp.arange(pairs, dtype=jnp.int32)[None, None, :]
    return jnp.sum(hit.astype(F32), axis=1)


def fused_kernel(
    n, cuts, amp_hbm, coef_hbm, ints_hbm, owner_hbm, local_hbm, coulomb_hbm, energy_hbm, out,
    amp, coef, ints, owner, local_index, coulomb, energy, counts,
    msg_out, msg_in, sum_out, sum_in, shuffle, halves, acc, other_counts, other_acc,
    load, msg_send, msg_recv, sum_send, sum_recv, aux_send, aux_recv,
):
    g, a = lax.axis_index("pairs"), lax.axis_index("aux")
    other = 1 - a
    pair_dev, width, _ = amp.shape
    pao = coef.shape[1]
    rows = pao // 2
    band = rows // n
    own = coulomb.shape[0]
    count_tiles = counts.shape[0]
    spans = ((0, count_tiles + band), (count_tiles + band, band))

    loads = [
        pltpu.make_async_copy(src, dst, load.at[i])
        for i, (src, dst) in enumerate(
            (
                (amp_hbm, amp), (coef_hbm, coef), (owner_hbm, owner), (local_hbm, local_index),
                (ints_hbm, ints), (coulomb_hbm, coulomb), (energy_hbm, energy),
            )
        )
    ]
    for copy in loads:
        copy.start()

    def partner(k):
        return lax.rem(g + lax.rem(k + n // 2 - 1, n - 1) + 1, n)

    barrier = pltpu.get_barrier_semaphore()

    def greet(k, _):
        pl.semaphore_signal(barrier, inc=1, device_id=(partner(k), a), device_id_type=MESH)
        return 0

    lax.fori_loop(1, n, greet, 0)
    pl.semaphore_signal(barrier, inc=1, device_id=(g, other), device_id_type=MESH)
    for copy in loads[:4]:
        copy.wait()

    mine = pl.ds(pl.multiple_of(a * rows, rows), rows)

    def backproject(q, _):
        half = dot(coef[q, mine, :], amp[q]).astype(BF)
        m = dot(half, coef[q], ((1,), (1,)))
        for side in range(2):
            start = pl.multiple_of((q * 2 + side) * rows, rows)
            shuffle[pl.ds(start, rows), :] = m[:, side * LANES:(side + 1) * LANES]
        return 0

    slots = owner.shape[1]
    per_pair = slots // pair_dev
    target = owner[...] * pair_dev + local_index[...]
    hit = lax.broadcasted_iota(jnp.int32, (n * pair_dev, slots), 0) == target
    first_slot = lax.broadcasted_iota(jnp.int32, (pair_dev, slots), 0) * per_pair
    slot = lax.broadcasted_iota(jnp.int32, (pair_dev, slots), 1)
    own_slot = (slot >= first_slot) & (slot < first_slot + per_pair)
    found = dot(
        jnp.where(own_slot, 1.0, 0.0).astype(BF), jnp.where(hit, 1.0, 0.0).astype(BF), ((1,), (1,))
    ).astype(BF)
    for j in range(count_tiles):
        counts[j] = found[:, j * LANES:(j + 1) * LANES]

    lax.fori_loop(0, pair_dev // 2, backproject, 0, unroll=4)
    pl.semaphore_wait(barrier, n)
    swap = pltpu.make_async_remote_copy(
        src_ref=counts, dst_ref=other_counts, send_sem=aux_send.at[0], recv_sem=aux_recv.at[0],
        device_id=(g, other), device_id_type=MESH,
    )
    swap.start()
    lax.fori_loop(pair_dev // 2, pair_dev, backproject, 0, unroll=4)
    swap.wait()
    all_counts = counts[...] + other_counts[...]

    def pack(h, side):
        for r in range(band):
            tile = shuffle[pl.ds(side * rows + h * band + r, pair_dev, stride=2 * rows), :]
            msg_out[h, count_tiles + side * band + r] = tile.astype(BF)
        if side == 0:
            msg_out[h, :count_tiles] = all_counts

    def message(side, h, slot):
        part = pl.ds(*spans[side])
        return pltpu.make_async_remote_copy(
            src_ref=msg_out.at[h, part], dst_ref=msg_in.at[slot, part],
            send_sem=msg_send.at[side, h], recv_sem=msg_recv.at[side, slot],
            device_id=(h, a), device_id_type=MESH,
        )

    def sums(side, h, slot):
        part = pl.ds(side * band, band)
        return pltpu.make_async_remote_copy(
            src_ref=sum_out.at[h, part], dst_ref=sum_in.at[slot, part],
            send_sem=sum_send.at[side, h], recv_sem=sum_recv.at[side, slot],
            device_id=(h, a), device_id_type=MESH,
        )

    def ship(side, k, _):
        h = partner(k)
        pack(h, side)
        message(side, h, g).start()
        return 0

    for side in range(2):
        lax.fori_loop(1, n, functools.partial(ship, side), 0)
    for side in range(2):
        pack(g, side)
    msg_in[g] = msg_out[g]

    acc[...] = jnp.zeros_like(acc)
    for copy in loads[4:]:
        copy.wait()

    def ladder(step, _):
        block = ints[pl.ds(step * CHUNK, CHUNK)]
        stacked = block.reshape(CHUNK * width, width)
        flipped = jnp.concatenate([block[j].T for j in range(CHUNK)], axis=0)
        for b in range(pair_dev // BLOCK):
            for p in range(0, BLOCK, 2):
                two = jnp.concatenate([amp[b * BLOCK + p], amp[b * BLOCK + p + 1]], axis=1)
                half = dot(stacked, two).astype(BF)
                for i in range(2):
                    for j in range(CHUNK):
                        halves[b, (p + i) * width:(p + i + 1) * width, j * width:(j + 1) * width] = (
                            half[j * width:(j + 1) * width, i * width:(i + 1) * width]
                        )
            acc[b * BLOCK:(b + 1) * BLOCK] += dot(halves[b], flipped).reshape(BLOCK, width, width)
        return 0

    def take_messages(side):
        def take(k, _):
            message(side, partner(k), partner(k)).wait_recv()
            return 0

        lax.fori_loop(1, n, take, 0)

    def add_up(side):
        matrix = jnp.concatenate(
            [msg_in[:, j].reshape(n * pair_dev, LANES) for j in range(count_tiles)], axis=1
        )
        for t in range(side * band, (side + 1) * band, 2):
            both = jnp.concatenate(
                [msg_in[:, count_tiles + t + j].reshape(n * pair_dev, LANES) for j in range(2)],
                axis=1,
            )
            total = dot(matrix, both).astype(BF)
            for j in range(2):
                sum_out[:, t + j] = total[:, j * LANES:(j + 1) * LANES].reshape(n, pair_dev, LANES)

        def ship_sums(k, _):
            sums(side, partner(k), g).start()
            return 0

        lax.fori_loop(1, n, ship_sums, 0)

    start = 0
    for side in range(2):
        lax.fori_loop(start, cuts[side], ladder, 0)
        start = cuts[side]
        take_messages(side)
        add_up(side)
    sum_in[g] = sum_out[g]

    def receive_sums(side):
        def take_sums(k, _):
            sums(side, partner(k), partner(k)).wait_recv()
            return 0

        lax.fori_loop(1, n, take_sums, 0)

        def spread(h, _):
            place = pl.multiple_of((side * n + h) * band * pair_dev, band * pair_dev)
            part = sum_in[h, side * band:(side + 1) * band]
            shuffle[pl.ds(place, band * pair_dev), :] = part.reshape(band * pair_dev, LANES).astype(F32)
            return 0

        lax.fori_loop(0, n, spread, 0, unroll=4)

    def project(side, p):
        s = shuffle[pl.ds(side * rows * pair_dev + p, rows, stride=pair_dev), :].astype(BF)
        y = dot(s, coef[p, side * LANES:(side + 1) * LANES, :]).astype(BF)
        acc[p] += dot(coef[p, mine, :], y, ((0,), (0,)))

    lax.fori_loop(start, cuts[2], ladder, 0)
    receive_sums(0)
    for p in range(pair_dev):
        project(0, p)
    lax.fori_loop(cuts[2], cuts[3], ladder, 0)
    receive_sums(1)

    for j in range(own):
        project(1, other * own + j)
    trade = pltpu.make_async_remote_copy(
        src_ref=acc.at[pl.ds(other * own, own)], dst_ref=other_acc, send_sem=aux_send.at[1],
        recv_sem=aux_recv.at[1], device_id=(g, other), device_id_type=MESH,
    )
    trade.start()
    for j in range(own):
        project(1, a * own + j)
    trade.wait()

    for i in range(own):
        residual = coulomb[i].astype(F32) + (acc[a * own + i] + other_acc[i])
        line = jnp.broadcast_to(energy[i:i + 1, :], (width, width))
        out[i] = amp[a * own + i].astype(F32) - residual / (line + line.T)

    for side in range(2):
        def finish(k, _):
            message(side, partner(k), g).wait_send()
            sums(side, partner(k), g).wait_send()
            return 0

        lax.fori_loop(1, n, finish, 0)


def fused(amplitudes, pno_coef, ladder_ints, coulomb_ints, pno_energy, link_owner, link_local):
    n = lax.axis_size("pairs")
    pair_dev, width, _ = amplitudes.shape
    pao = pno_coef.shape[1]
    pairs = n * pair_dev
    count_tiles = pairs // LANES
    band = pao // 2 // n
    tiles = 2 * band
    own = coulomb_ints.shape[0]
    steps = ladder_ints.shape[0] // CHUNK
    operands = (
        amplitudes, pno_coef, ladder_ints, link_owner.reshape(1, -1), link_local.reshape(1, -1),
        coulomb_ints, pno_energy,
    )
    return pl.pallas_call(
        functools.partial(fused_kernel, n, (steps // 4, steps // 2, 17 * steps // 20, steps)),
        out_shape=jax.ShapeDtypeStruct(coulomb_ints.shape, F32),
        in_specs=[pl.BlockSpec(memory_space=pl.ANY)] * len(operands),
        out_specs=pl.BlockSpec(memory_space=pltpu.VMEM),
        scratch_shapes=[
            *(pltpu.VMEM(x.shape, x.dtype) for x in operands),
            pltpu.VMEM((count_tiles, pair_dev, LANES), BF),
            pltpu.VMEM((n, tiles + count_tiles, pair_dev, LANES), BF),
            pltpu.VMEM((n, tiles + count_tiles, pair_dev, LANES), BF),
            pltpu.VMEM((n, tiles, pair_dev, LANES), BF),
            pltpu.VMEM((n, tiles, pair_dev, LANES), BF),
            pltpu.VMEM((pair_dev * pao, LANES), F32),
            pltpu.VMEM((pair_dev // BLOCK, BLOCK * width, CHUNK * width), BF),
            pltpu.VMEM((pair_dev, width, width), F32),
            pltpu.VMEM((count_tiles, pair_dev, LANES), BF),
            pltpu.VMEM((own, width, width), F32),
            pltpu.SemaphoreType.DMA((len(operands),)),
            pltpu.SemaphoreType.DMA((2, n)),
            pltpu.SemaphoreType.DMA((2, n)),
            pltpu.SemaphoreType.DMA((2, n)),
            pltpu.SemaphoreType.DMA((2, n)),
            pltpu.SemaphoreType.DMA((2,)),
            pltpu.SemaphoreType.DMA((2,)),
        ],
        compiler_params=pltpu.CompilerParams(
            collective_id=0, has_side_effects=True, vmem_limit_bytes=60 * 2**20
        ),
    )(*operands)


def general(amplitudes, pno_coef, ladder_ints, coulomb_ints, pno_energy, link_owner, link_local):
    groups, parts = lax.axis_size("pairs"), lax.axis_size("aux")
    devices = groups * parts
    pair_dev, width, _ = amplitudes.shape
    pao = pno_coef.shape[1]
    own = coulomb_ints.shape[0]
    first = lax.axis_index("aux") * own
    both = ("pairs", "aux")
    counts = link_counts(link_owner, link_local, pair_dev, groups * pair_dev)
    matrix = lax.all_gather(lax.psum(counts, "aux"), "pairs", axis=0, tiled=True).astype(BF)
    amp = lax.dynamic_slice_in_dim(amplitudes, first, own, 0)
    coef = lax.dynamic_slice_in_dim(pno_coef, first, own, 0)
    half = jnp.einsum("qac,qcd->qad", coef, amp, preferred_element_type=F32).astype(BF)
    back = jnp.einsum("qad,qbd->qab", half, coef, preferred_element_type=F32).astype(BF)
    back = jnp.swapaxes(back.reshape(own, devices, -1), 0, 1)
    back = lax.all_to_all(back, both, split_axis=0, concat_axis=0, tiled=True)
    total = dot(matrix, back.reshape(devices * own, -1)).astype(BF)
    total = lax.all_to_all(
        total.reshape(devices, own, -1), both, split_axis=0, concat_axis=0, tiled=True
    )
    total = jnp.swapaxes(total, 0, 1).reshape(own, pao, pao)
    near = jnp.einsum("pab,pbd->pad", total, coef, preferred_element_type=F32).astype(BF)
    linked = jnp.einsum("pac,pad->pcd", coef, near, preferred_element_type=F32)

    def ladder_terms(amp_p):
        ladder_half = jnp.einsum(
            "qcd,de->qce", ladder_ints, amp_p, preferred_element_type=F32
        ).astype(BF)
        return jnp.einsum("qce,qfe->cf", ladder_half, ladder_ints, preferred_element_type=F32)

    ladder = lax.psum_scatter(
        lax.map(ladder_terms, amplitudes), "aux", scatter_dimension=0, tiled=True
    )
    residual = coulomb_ints.astype(F32) + ladder + linked
    denominator = pno_energy[:, :, None] + pno_energy[:, None, :]
    return amp.astype(F32) - residual / denominator


def local(*arrays):
    amplitudes, pno_coef, ladder_ints = arrays[:3]
    n = lax.axis_size("pairs")
    fits = (
        lax.axis_size("aux") == 2
        and amplitudes.shape[1] == LANES
        and pno_coef.shape[1] == 2 * LANES
        and amplitudes.shape[0] == 16
        and LANES % (8 * n) == 0
        and n * 16 % LANES == 0
        and ladder_ints.shape[0] % CHUNK == 0
    )
    return fused(*arrays) if fits else general(*arrays)


def solution(mesh):
    in_specs = (
        P("pairs", None, None),
        P("pairs", None, None),
        P("aux", None, None),
        P(("pairs", "aux"), None, None),
        P(("pairs", "aux"), None),
        P(("pairs", "aux"), None),
        P(("pairs", "aux"), None),
    )
    out_specs = P(("pairs", "aux"), None, None)
    return jax.shard_map(local, mesh=mesh, in_specs=in_specs, out_specs=out_specs, check_vma=False)
```

```python
import functools

import jax
import jax.numpy as jnp
from jax import lax
from jax.experimental import pallas as pl
from jax.experimental.pallas import tpu as pltpu
from jax.sharding import PartitionSpec as P

MESH = pl.DeviceIdType.MESH
BF = jnp.bfloat16
F32 = jnp.float32
LANES = 128
CHUNK = 4
BLOCK = 8


def dot(x, y, dims=((1,), (0,))):
    return lax.dot_general(x, y, (dims, ((), ())), preferred_element_type=F32)


def link_counts(link_owner, link_local, pair_dev, pairs):
    target = (link_owner * pair_dev + link_local).reshape(pair_dev, -1, 1)
    hit = target == jnp.arange(pairs, dtype=jnp.int32)[None, None, :]
    return jnp.sum(hit.astype(F32), axis=1)


def fused_kernel(
    n, cuts, amp_hbm, coef_hbm, ints_hbm, owner_hbm, local_hbm, coulomb_hbm, energy_hbm, out,
    amp, coef, ints, owner, local_index, coulomb, energy, counts,
    msg_out, msg_in, sum_out, sum_in, shuffle, acc, other_counts, other_acc,
    load, msg_send, msg_recv, sum_send, sum_recv, aux_send, aux_recv,
):
    g, a = lax.axis_index("pairs"), lax.axis_index("aux")
    other = 1 - a
    pair_dev, width, _ = amp.shape
    pao = coef.shape[1]
    rows = pao // 2
    band = rows // n
    own = coulomb.shape[0]
    count_tiles = counts.shape[0]
    spans = ((0, count_tiles + band), (count_tiles + band, band))

    loads = [
        pltpu.make_async_copy(src, dst, load.at[i])
        for i, (src, dst) in enumerate(
            (
                (amp_hbm, amp), (coef_hbm, coef), (owner_hbm, owner), (local_hbm, local_index),
                (ints_hbm, ints), (coulomb_hbm, coulomb), (energy_hbm, energy),
            )
        )
    ]
    for copy in loads:
        copy.start()

    def partner(k):
        return lax.rem(g + lax.rem(k + n // 2 - 1, n - 1) + 1, n)

    barrier = pltpu.get_barrier_semaphore()

    def greet(k, _):
        pl.semaphore_signal(barrier, inc=1, device_id=(partner(k), a), device_id_type=MESH)
        return 0

    lax.fori_loop(1, n, greet, 0)
    pl.semaphore_signal(barrier, inc=1, device_id=(g, other), device_id_type=MESH)
    for copy in loads[:4]:
        copy.wait()

    mine = pl.ds(pl.multiple_of(a * rows, rows), rows)

    def backproject(q, _):
        half = dot(coef[q, mine, :], amp[q]).astype(BF)
        m = dot(half, coef[q], ((1,), (1,)))
        for side in range(2):
            start = pl.multiple_of((q * 2 + side) * rows, rows)
            shuffle[pl.ds(start, rows), :] = m[:, side * LANES:(side + 1) * LANES]
        return 0

    slots = owner.shape[1]
    per_pair = slots // pair_dev
    target = owner[...] * pair_dev + local_index[...]
    hit = lax.broadcasted_iota(jnp.int32, (n * pair_dev, slots), 0) == target
    first_slot = lax.broadcasted_iota(jnp.int32, (pair_dev, slots), 0) * per_pair
    slot = lax.broadcasted_iota(jnp.int32, (pair_dev, slots), 1)
    own_slot = (slot >= first_slot) & (slot < first_slot + per_pair)
    found = dot(
        jnp.where(own_slot, 1.0, 0.0).astype(BF), jnp.where(hit, 1.0, 0.0).astype(BF), ((1,), (1,))
    ).astype(BF)
    for j in range(count_tiles):
        counts[j] = found[:, j * LANES:(j + 1) * LANES]

    lax.fori_loop(0, pair_dev // 2, backproject, 0, unroll=4)
    def ladder(step, _):
        block = ints[pl.ds(step * CHUNK, CHUNK)]
        flipped = jnp.concatenate([block[j].T for j in range(CHUNK)], axis=1)
        wide = jnp.concatenate([block[j] for j in range(CHUNK)], axis=1)

        def first(b):
            group = amp[BLOCK * b:BLOCK * (b + 1)].reshape(BLOCK * width, width)
            return dot(group, flipped).astype(BF)

        half = first(0)
        for b in range(pair_dev // BLOCK):
            coming = first(b + 1) if b + 1 < pair_dev // BLOCK else None
            for pp in range(BLOCK // 2):
                turned = jnp.concatenate(
                    [
                        jnp.concatenate(
                            [
                                half[i * width:(i + 1) * width, j * width:(j + 1) * width]
                                for i in (2 * pp, 2 * pp + 1)
                            ],
                            axis=1,
                        )
                        for j in range(CHUNK)
                    ],
                    axis=0,
                )
                acc[BLOCK // 2 * b + pp] += dot(wide, turned)
            half = coming
        return 0

    acc[...] = jnp.zeros_like(acc)
    for copy in loads[4:]:
        copy.wait()
    lax.fori_loop(0, cuts[0], ladder, 0)
    pl.semaphore_wait(barrier, n)
    swap = pltpu.make_async_remote_copy(
        src_ref=counts, dst_ref=other_counts, send_sem=aux_send.at[0], recv_sem=aux_recv.at[0],
        device_id=(g, other), device_id_type=MESH,
    )
    swap.start()
    lax.fori_loop(pair_dev // 2, pair_dev, backproject, 0, unroll=4)
    swap.wait()
    all_counts = counts[...] + other_counts[...]

    def pack(h, side):
        for r in range(band):
            tile = shuffle[pl.ds(side * rows + h * band + r, pair_dev, stride=2 * rows), :]
            msg_out[h, count_tiles + side * band + r] = tile.astype(BF)
        if side == 0:
            msg_out[h, :count_tiles] = all_counts

    def message(side, h, slot):
        part = pl.ds(*spans[side])
        return pltpu.make_async_remote_copy(
            src_ref=msg_out.at[h, part], dst_ref=msg_in.at[slot, part],
            send_sem=msg_send.at[side, h], recv_sem=msg_recv.at[side, slot],
            device_id=(h, a), device_id_type=MESH,
        )

    def sums(side, h, slot):
        part = pl.ds(side * band, band)
        return pltpu.make_async_remote_copy(
            src_ref=sum_out.at[h, part], dst_ref=sum_in.at[slot, part],
            send_sem=sum_send.at[side, h], recv_sem=sum_recv.at[side, slot],
            device_id=(h, a), device_id_type=MESH,
        )

    def ship(side, k, _):
        h = partner(k)
        pack(h, side)
        message(side, h, g).start()
        return 0

    for side in range(2):
        lax.fori_loop(1, n, functools.partial(ship, side), 0)
    for side in range(2):
        pack(g, side)
    msg_in[g] = msg_out[g]

    def take_messages(side):
        def take(k, _):
            message(side, partner(k), partner(k)).wait_recv()
            return 0

        lax.fori_loop(1, n, take, 0)

    def add_up(side):
        matrix = jnp.concatenate(
            [msg_in[:, j].reshape(n * pair_dev, LANES) for j in range(count_tiles)], axis=1
        )
        for t in range(side * band, (side + 1) * band, 2):
            both = jnp.concatenate(
                [msg_in[:, count_tiles + t + j].reshape(n * pair_dev, LANES) for j in range(2)],
                axis=1,
            )
            total = dot(matrix, both).astype(BF)
            for j in range(2):
                sum_out[:, t + j] = total[:, j * LANES:(j + 1) * LANES].reshape(n, pair_dev, LANES)

        def ship_sums(k, _):
            sums(side, partner(k), g).start()
            return 0

        lax.fori_loop(1, n, ship_sums, 0)

    for side in range(2):
        lax.fori_loop(cuts[side], cuts[side + 1], ladder, 0)
        take_messages(side)
        add_up(side)
    sum_in[g] = sum_out[g]

    def receive_sums(side):
        def take_sums(k, _):
            sums(side, partner(k), partner(k)).wait_recv()
            return 0

        lax.fori_loop(1, n, take_sums, 0)

        def spread(h, _):
            place = pl.multiple_of((side * n + h) * band * pair_dev, band * pair_dev)
            part = sum_in[h, side * band:(side + 1) * band]
            shuffle[pl.ds(place, band * pair_dev), :] = part.reshape(band * pair_dev, LANES).astype(F32)
            return 0

        lax.fori_loop(0, n, spread, 0, unroll=4)

    def project(side, pp):
        found = []
        for i in range(2):
            p = 2 * pp + i
            s = shuffle[pl.ds(side * rows * pair_dev + p, rows, stride=pair_dev), :].astype(BF)
            y = dot(s, coef[p, side * LANES:(side + 1) * LANES, :]).astype(BF)
            found.append(dot(coef[p, mine, :], y, ((0,), (0,))))
        acc[pp] += jnp.concatenate(found, axis=1)

    lax.fori_loop(cuts[2], cuts[3], ladder, 0)
    receive_sums(0)
    for pp in range(pair_dev // 2):
        project(0, pp)
    lax.fori_loop(cuts[3], cuts[4], ladder, 0)
    receive_sums(1)

    few = own // 2
    for j in range(few):
        project(1, other * few + j)
    trade = pltpu.make_async_remote_copy(
        src_ref=acc.at[pl.ds(other * few, few)], dst_ref=other_acc, send_sem=aux_send.at[1],
        recv_sem=aux_recv.at[1], device_id=(g, other), device_id_type=MESH,
    )
    trade.start()
    for j in range(few):
        project(1, a * few + j)
    trade.wait()

    for i in range(own):
        lanes = slice((i % 2) * width, (i % 2 + 1) * width)
        reduced = acc[a * few + i // 2, :, lanes] + other_acc[i // 2, :, lanes]
        residual = coulomb[i].astype(F32) + reduced
        line = jnp.broadcast_to(energy[i:i + 1, :], (width, width))
        out[i] = amp[a * own + i].astype(F32) - residual / (line + line.T)

    for side in range(2):
        def finish(k, _):
            message(side, partner(k), g).wait_send()
            sums(side, partner(k), g).wait_send()
            return 0

        lax.fori_loop(1, n, finish, 0)


def fused(amplitudes, pno_coef, ladder_ints, coulomb_ints, pno_energy, link_owner, link_local):
    n = lax.axis_size("pairs")
    pair_dev, width, _ = amplitudes.shape
    pao = pno_coef.shape[1]
    pairs = n * pair_dev
    count_tiles = pairs // LANES
    band = pao // 2 // n
    tiles = 2 * band
    own = coulomb_ints.shape[0]
    steps = ladder_ints.shape[0] // CHUNK
    operands = (
        amplitudes, pno_coef, ladder_ints, link_owner.reshape(1, -1), link_local.reshape(1, -1),
        coulomb_ints, pno_energy,
    )
    return pl.pallas_call(
        functools.partial(fused_kernel, n, (steps // 10, 11 * steps // 40, steps // 2, 17 * steps // 20, steps)),
        out_shape=jax.ShapeDtypeStruct(coulomb_ints.shape, F32),
        in_specs=[pl.BlockSpec(memory_space=pl.ANY)] * len(operands),
        out_specs=pl.BlockSpec(memory_space=pltpu.VMEM),
        scratch_shapes=[
            *(pltpu.VMEM(x.shape, x.dtype) for x in operands),
            pltpu.VMEM((count_tiles, pair_dev, LANES), BF),
            pltpu.VMEM((n, tiles + count_tiles, pair_dev, LANES), BF),
            pltpu.VMEM((n, tiles + count_tiles, pair_dev, LANES), BF),
            pltpu.VMEM((n, tiles, pair_dev, LANES), BF),
            pltpu.VMEM((n, tiles, pair_dev, LANES), BF),
            pltpu.VMEM((pair_dev * pao, LANES), F32),
            pltpu.VMEM((pair_dev // 2, width, 2 * width), F32),
            pltpu.VMEM((count_tiles, pair_dev, LANES), BF),
            pltpu.VMEM((own // 2, width, 2 * width), F32),
            pltpu.SemaphoreType.DMA((len(operands),)),
            pltpu.SemaphoreType.DMA((2, n)),
            pltpu.SemaphoreType.DMA((2, n)),
            pltpu.SemaphoreType.DMA((2, n)),
            pltpu.SemaphoreType.DMA((2, n)),
            pltpu.SemaphoreType.DMA((2,)),
            pltpu.SemaphoreType.DMA((2,)),
        ],
        compiler_params=pltpu.CompilerParams(
            collective_id=0, has_side_effects=True, vmem_limit_bytes=60 * 2**20
        ),
    )(*operands)


def general(amplitudes, pno_coef, ladder_ints, coulomb_ints, pno_energy, link_owner, link_local):
    groups, parts = lax.axis_size("pairs"), lax.axis_size("aux")
    devices = groups * parts
    pair_dev, width, _ = amplitudes.shape
    pao = pno_coef.shape[1]
    own = coulomb_ints.shape[0]
    first = lax.axis_index("aux") * own
    both = ("pairs", "aux")
    counts = link_counts(link_owner, link_local, pair_dev, groups * pair_dev)
    matrix = lax.all_gather(lax.psum(counts, "aux"), "pairs", axis=0, tiled=True).astype(BF)
    amp = lax.dynamic_slice_in_dim(amplitudes, first, own, 0)
    coef = lax.dynamic_slice_in_dim(pno_coef, first, own, 0)
    half = jnp.einsum("qac,qcd->qad", coef, amp, preferred_element_type=F32).astype(BF)
    back = jnp.einsum("qad,qbd->qab", half, coef, preferred_element_type=F32).astype(BF)
    back = jnp.swapaxes(back.reshape(own, devices, -1), 0, 1)
    back = lax.all_to_all(back, both, split_axis=0, concat_axis=0, tiled=True)
    total = dot(matrix, back.reshape(devices * own, -1)).astype(BF)
    total = lax.all_to_all(
        total.reshape(devices, own, -1), both, split_axis=0, concat_axis=0, tiled=True
    )
    total = jnp.swapaxes(total, 0, 1).reshape(own, pao, pao)
    near = jnp.einsum("pab,pbd->pad", total, coef, preferred_element_type=F32).astype(BF)
    linked = jnp.einsum("pac,pad->pcd", coef, near, preferred_element_type=F32)

    def ladder_terms(amp_p):
        ladder_half = jnp.einsum(
            "qcd,de->qce", ladder_ints, amp_p, preferred_element_type=F32
        ).astype(BF)
        return jnp.einsum("qce,qfe->cf", ladder_half, ladder_ints, preferred_element_type=F32)

    ladder = lax.psum_scatter(
        lax.map(ladder_terms, amplitudes), "aux", scatter_dimension=0, tiled=True
    )
    residual = coulomb_ints.astype(F32) + ladder + linked
    denominator = pno_energy[:, :, None] + pno_energy[:, None, :]
    return amp.astype(F32) - residual / denominator


def local(*arrays):
    amplitudes, pno_coef, ladder_ints = arrays[:3]
    n = lax.axis_size("pairs")
    fits = (
        lax.axis_size("aux") == 2
        and amplitudes.shape[1] == LANES
        and pno_coef.shape[1] == 2 * LANES
        and amplitudes.shape[0] == 16
        and LANES % (8 * n) == 0
        and n * 16 % LANES == 0
        and ladder_ints.shape[0] % CHUNK == 0
    )
    return fused(*arrays) if fits else general(*arrays)


def solution(mesh):
    in_specs = (
        P("pairs", None, None),
        P("pairs", None, None),
        P("aux", None, None),
        P(("pairs", "aux"), None, None),
        P(("pairs", "aux"), None),
        P(("pairs", "aux"), None),
        P(("pairs", "aux"), None),
    )
    out_specs = P(("pairs", "aux"), None, None)
    return jax.shard_map(local, mesh=mesh, in_specs=in_specs, out_specs=out_specs, check_vma=False)
```
